32 devices in a mesh: walk: 8 (over z, core), chol: 4 (over y, x).
Axes of the slice: x: 2, y: 2, z: 4, core: 2. Of those that a mesh axis runs over, the one named last changes fastest.
Arguments:
- walkers: float32 [16, 512, 200], P('walk'), as said below
- cholesky: float32 [8, 512, 512], P('chol'), as said below
- fields: float32 [16, 8], P('walk', 'chol'), may hold values from -4 to 4
- weights: float32 [16], P('walk'), may hold values from 0.5 to 2
- counts: int32 [16], P('walk'), may hold values from 0 to 4, as said below
Outputs:
- routed: float32 [16, 512, 200], P('walk')
- comb_marks: float32 [16], P('walk')
The draws below stay inside these ranges and needn't reach their ends.
Inputs may be any that keep to these rules, and one draw needn't show every extreme that they name: The counts sum to 16. With end as in the reference program, the copies of walkers 2 * s to 2 * (s + 1) - 1 occupy new positions from 2 * (s - 1) to 2 * (s + 2) - 1. Some walker has 4 copies in every draw. `walkers`: for every walker the intersection matrix (its first 100 rows) differs from the identity by a matrix of spectral norm below one. `cholesky`: each vector is a symmetric matrix.
All inputs are finite; a program needn't handle non-finite values.
Results may differ from the reference program's by a relative error of at most 0.0001.
Values sent between devices are 32-bit elements; how exact they have to be, the bound alone decides.
No kernel may reach another device: no remote copies, remote signals or barrier semaphores. Data moves between devices by JAX's collectives and lax.ppermute only.
A program may use at most 64 MiB of HBM per device.

```python
import math
import jax
import jax.numpy as jnp
from jax import lax

NORB = 512
NELEC = 100
WALK_DEV = 2
TAYLOR = 3
NEWTON = 3
NCHOL = 8
WALKERS = 16


def draw_walkers(key, part):
    key_real, key_imag = jax.random.split(key)
    shape_full = (WALKERS, NORB, NELEC)
    noise_real = jax.random.normal(key_real, shape_full, jnp.float32)
    noise_imag = jax.random.normal(key_imag, shape_full, jnp.float32)
    small_scale = 0.2 * (2.0 * NELEC) ** (-0.5)
    row_ids = jnp.arange(NORB)[:, None]
    row_scale = jnp.where(row_ids < NELEC, small_scale, 0.05)
    identity = (row_ids == jnp.arange(NELEC)[None, :]).astype(jnp.float32)
    real_part = identity[None] + row_scale[None] * noise_real
    imag_part = row_scale[None] * noise_imag
    return jnp.concatenate([real_part, imag_part], axis=-1).astype(jnp.float32)


def draw_cholesky(key, part):
    key_noise, key_diag = jax.random.split(key)
    shape_full = (NCHOL, NORB, NORB)
    noise = jax.random.normal(key_noise, shape_full, jnp.float32)
    symmetric = (noise + jnp.swapaxes(noise, 1, 2)) * 0.5 ** 0.5
    sigma = 5.0 * (NCHOL * NORB) ** (-0.5)
    diagonal = jax.random.uniform(key_diag, (NCHOL,), jnp.float32, 0.5, 1.5) * (2.5 / NELEC)
    identity = jnp.eye(NORB, dtype=jnp.float32)
    return (sigma * symmetric + diagonal[:, None, None] * identity[None]).astype(jnp.float32)


def draw_counts(key, part):
    groups = WALKERS // WALK_DEV
    half_width = WALK_DEV // 2
    key_drift, key_slots = jax.random.split(key)
    drift = jax.random.randint(key_drift, (groups + 1,), -half_width, half_width + 1)
    edges = jnp.arange(groups + 1)
    drift = jnp.where(edges == 1, -half_width, drift)
    drift = jnp.where(edges == 2, half_width, drift)
    drift = jnp.where((edges == 0) | (edges == groups), 0, drift)
    copies_total = WALK_DEV + drift[1:] - drift[:-1]
    group_keys = jax.random.split(key_slots, groups)
    shuffled = jax.vmap(lambda group_key: jax.random.permutation(group_key, 4 * WALK_DEV))(group_keys)
    group_ids = jnp.arange(groups)[:, None]
    slot_ids = jnp.arange(4 * WALK_DEV)[None, :]
    scores = jnp.where((group_ids == 1) & (slot_ids < 4), slot_ids - 4, shuffled)
    ranking = jnp.argsort(scores, axis=1, stable=True)
    slot_rank = jnp.argsort(ranking, axis=1, stable=True)
    chosen = (slot_rank < copies_total[:, None]).astype(jnp.int32)
    counts = jnp.sum(chosen.reshape(groups, WALK_DEV, 4), axis=-1)
    return counts.reshape(WALKERS).astype(jnp.int32)


def shard_levels(rng, shape, pieces, low, top_value):
    def one(axis_at, parts):
        draws = jax.random.uniform(jax.random.fold_in(jax.random.fold_in(rng, 6), axis_at), (parts,), jnp.float32, low / len(pieces), top_value / len(pieces))
        return jnp.repeat(jnp.exp(draws), shape[axis_at] // parts).reshape((-1,) + (1,) * (len(shape) - axis_at - 1))

    gain = one(*pieces[0])
    for cut in pieces[1:]:
        gain = gain * one(*cut)
    return gain


def scatter_about(own_key, dims, deviation, bound, cuts=(), kind=jnp.bfloat16):
    values = jax.random.normal(own_key, dims, jnp.float32) * deviation
    if len(cuts) > 0:
        values = shard_levels(own_key, dims, cuts, -0.22, 0.18) * values
    return jnp.clip(values, min=-bound, max=bound).astype(kind)


def setup_inputs(seed: int = 0) -> dict:
    seeds = jax.random.split(jax.random.key(seed), 6)
    return {
        "walkers": draw_walkers(jax.random.fold_in(seeds[5], 71), 0),
        "cholesky": draw_cholesky(jax.random.fold_in(seeds[5], 71), 0),
        "fields": scatter_about(seeds[2], (WALKERS, NCHOL), 1.0, 4.0, ((0, 8), (1, 4)), jnp.float32),
        "weights": jnp.clip(jnp.exp(math.log(2.0) - 1.3862944 * jax.random.uniform(seeds[3], (WALKERS,), jnp.float32) ** shard_levels(seeds[3], (WALKERS,), ((0, 8),), -0.2, 0.2)), 0.5, 2.0),
        "counts": draw_counts(jax.random.fold_in(seeds[5], 71), 0),
    }


highest = lax.Precision.HIGHEST
root_dt = 0.1


def rotate(block):
    half_width = block.shape[-1] // 2
    return jnp.concatenate([-block[..., half_width:], block[..., :half_width]], axis=-1)


def complex_product(left_real, left_imag, right_real, right_imag):
    real_part = jnp.dot(left_real, right_real, precision=highest) - jnp.dot(left_imag, right_imag, precision=highest)
    imag_part = jnp.dot(left_real, right_imag, precision=highest) + jnp.dot(left_imag, right_real, precision=highest)
    return real_part, imag_part


def intersection_inverse(over_real, over_imag):
    identity = jnp.eye(over_real.shape[0], dtype=over_real.dtype)
    inv_real = identity
    inv_imag = jnp.zeros_like(identity)
    for sweep_step in range(NEWTON):
        prod_real, prod_imag = complex_product(over_real, over_imag, inv_real, inv_imag)
        inv_real, inv_imag = complex_product(inv_real, inv_imag, 2.0 * identity - prod_real, -prod_imag)
    return inv_real, inv_imag


def propagate(walker, fields_row, cholesky):
    walk_real = walker[:, :NELEC]
    walk_imag = walker[:, NELEC:]
    inv_real, inv_imag = intersection_inverse(walk_real[:NELEC], walk_imag[:NELEC])
    theta_real, theta_imag = complex_product(walk_real, walk_imag, inv_real, inv_imag)
    top_rows = cholesky[:, :NELEC, :]
    force_real = root_dt * jnp.einsum('gak,ka->g', top_rows, theta_real, precision=highest)
    force_imag = root_dt * jnp.einsum('gak,ka->g', top_rows, theta_imag, precision=highest)
    coeff_real = root_dt * force_imag
    coeff_imag = root_dt * (fields_row - force_real)
    oper_real = jnp.tensordot(coeff_real, cholesky, axes=1, precision=highest)
    oper_imag = jnp.tensordot(coeff_imag, cholesky, axes=1, precision=highest)
    taylor_term = walker
    series = walker
    for degree in range(1, TAYLOR + 1):
        taylor_term = (jnp.dot(oper_real, taylor_term, precision=highest) + jnp.dot(oper_imag, rotate(taylor_term), precision=highest)) / degree
        series = series + taylor_term
    log_weight = jnp.sum(fields_row * force_real - 0.5 * (force_real * force_real - force_imag * force_imag))
    return series, log_weight


def reference(walkers, cholesky, fields, weights, counts):
    def per_walker(walker_pair):
        return propagate(walker_pair[0], walker_pair[1], cholesky)

    propagated, log_weight = lax.map(per_walker, (walkers, fields))
    new_weights = weights * jnp.exp(log_weight)
    running = jnp.cumsum(new_weights)
    comb_marks = WALKERS * running / running[-1]
    end_marks = jnp.cumsum(counts).astype(jnp.int32)
    position = jnp.arange(WALKERS, dtype=jnp.int32)
    source = jnp.sum((end_marks[None, :] <= position[:, None]).astype(jnp.int32), axis=1).astype(jnp.int32)
    routed = jnp.take(propagated, source, axis=0)
    return routed, comb_marks
```

```python
import functools
import jax
import jax.numpy as jnp
from jax import lax
from jax.experimental import pallas as pl
from jax.experimental.pallas import tpu as pltpu
from jax.sharding import PartitionSpec as P

TAYLOR = 3
NEWTON = 3
CORES = 2
ROOT_DT = 0.1

f32 = jnp.float32
highest = lax.Precision.HIGHEST
VMEM = pl.BlockSpec(memory_space=pltpu.VMEM)
SMEM = pl.BlockSpec(memory_space=pltpu.SMEM)
PARAMS = pltpu.CompilerParams(vmem_limit_bytes=48 * 2**20)


def dot(left, right, precision=None):
    return jnp.dot(left, right, precision=precision, preferred_element_type=f32)


def ids(rows, columns):
    shape = (rows, columns)
    return (
        lax.broadcasted_iota(jnp.int32, shape, 0),
        lax.broadcasted_iota(jnp.int32, shape, 1),
    )


def up_to(n, unit):
    return -(-n // unit) * unit


def packed(vectors, which):
    m = vectors.shape[1] // 2
    i, j = ids(m, m)
    both = jnp.where(i <= j, vectors[:, :m, :m], vectors[:, m:, m:])
    return jnp.where(which == 0, both, vectors[:, :m, m:])


def prep_kernel(fields, walk, vec, small, other, full, parity):
    count, width, norb = walk.shape
    half = norb // 2
    nelec = width // 2
    pad = up_to(nelec, 128)
    nvec = vec.shape[0]
    i, j = ids(2 * pad, 2 * pad)
    eye = jnp.where((i == j) & (i % pad < nelec), 1.0, 0.0).astype(f32)
    full[...] = jnp.zeros_like(full)
    lane = lax.broadcasted_iota(jnp.int32, (1, small.shape[1]), 1)
    row = jnp.zeros((1, small.shape[1]), f32)
    inside = lax.broadcasted_iota(jnp.int32, (pad, pad), 1) < nelec
    rows = up_to(nelec, 8)
    for w in range(count):
        full[w, :nelec] = walk[w, :nelec]
        full[w, pad : pad + nelec] = walk[w, nelec:]
        over_real = jnp.where(inside, full[w, :pad, :pad], 0.0)
        over_imag = jnp.where(inside, full[w, pad:, :pad], 0.0)
        over = jnp.concatenate(
            [
                jnp.concatenate([over_real, -over_imag], axis=1),
                jnp.concatenate([over_imag, over_real], axis=1),
            ],
            axis=0,
        )
        inv = 2.0 * eye - over
        for _ in range(NEWTON - 1):
            inv = dot(2.0 * eye - dot(inv, over, highest), inv, highest)
        theta = dot(inv, full[w], highest)
        log_part = jnp.zeros((1, 1), f32)
        for g in range(nvec):
            top = vec[g, :rows, :]
            xr = ROOT_DT * jnp.sum(top * theta[:rows], keepdims=True)
            xi = ROOT_DT * jnp.sum(top * theta[pad : pad + rows], keepdims=True)
            field = fields[w, g]
            at = 2 * (w * nvec + g)
            row += jnp.where(lane == at, ROOT_DT * xi, 0.0)
            row += jnp.where(lane == at + 1, ROOT_DT * (field - xr), 0.0)
            log_part += field * xr - 0.5 * (xr * xr - xi * xi)
        row += jnp.where(lane == 2 * count * nvec + w, log_part, 0.0)
    small[...] = jnp.zeros_like(small)
    small[0:1] = row
    i, j = ids(half, half)
    for g in range(nvec):
        corner = vec[g, half:, half:]
        small[g + 1 : g + 2] = jnp.sum(jnp.where(i == j, corner, 0.0), axis=0, keepdims=True)

    @pl.when(parity[0] == 0)
    def _():
        other[...] = vec[:, :half, half:]

    @pl.when(parity[0] != 0)
    def _():
        for g in range(nvec):
            other[g] = jnp.where(i <= j, vec[g, :half, :half], vec[g, half:, half:])


def group_kernel(count, nvec, weights, counts, *refs):
    smalls, out = refs[:-1], refs[-1]
    width = out.shape[1]
    lane = lax.broadcasted_iota(jnp.int32, (1, width), 1)
    per = 2 * count * nvec
    logs = smalls[0][0:1]
    for s in smalls[1:]:
        logs = logs + s[0:1]
    row = jnp.zeros((1, width), f32)
    for k, s in enumerate(smalls):
        mine = jnp.where(lane < per, s[0:1], 0.0)
        row += mine if k == 0 else pltpu.roll(mine, k * per, 1)
    base = per * len(smalls)
    for w in range(count):
        log_weight = jnp.sum(jnp.where(lane == per + w, logs, 0.0), axis=1, keepdims=True)
        row += jnp.where(lane == base + w, weights[w] * jnp.exp(log_weight), 0.0)
        row += jnp.where(lane == base + count + w, counts[w].astype(f32), 0.0)
    out[...] = row


def final_kernel(count, nvec, slots, zs, where_at, *refs):
    refs = list(refs)

    def take(n):
        head = refs[:n]
        del refs[:n]
        return head

    rows = take(zs)
    walks = take(3)
    smalls = take(slots)
    mine = [take(2) for _ in range(slots)]
    theirs = [take(2) for _ in range(slots)]
    out, marks, acc, a_hi, a_lo, source = refs
    me, core = where_at[0], where_at[1]
    z = me // CORES
    per = 2 * count * nvec
    base = per * slots
    width = walks[0].shape[1]
    nelec = width // 2
    norb = walks[0].shape[2]
    half = norb // 2
    part = half // 2
    pad = up_to(nelec, 16)

    total = jnp.float32(0.0)
    before = jnp.float32(0.0)
    base_count = jnp.float32(0.0)
    for k in range(zs):
        for r in range(CORES):
            there = CORES * lax.rem(z - k + zs, zs) + (core if r == 0 else CORES - 1 - core)
            earlier = (there < me).astype(f32)
            for w in range(count):
                weight = rows[k][r, base + w]
                total += weight
                before += earlier * weight
                base_count += earlier * rows[k][r, base + count + w]
    lane = lax.broadcasted_iota(jnp.int32, marks.shape, 1)
    mark_row = jnp.zeros(marks.shape, f32)
    for w in range(count):
        before += rows[0][0, base + w]
        mark_row += jnp.where(lane == w, before, 0.0)
    factor = jnp.full(marks.shape, total, f32)
    marks[...] = (CORES * zs * count) * mark_row / factor

    def behind(at):
        return jnp.where(core == 0, rows[1 % zs][1, at], rows[0][1, at])

    def here(at):
        return rows[0][0, at]

    def ahead(at):
        return jnp.where(core == 0, rows[0][1, at], rows[zs - 1][1, at])

    groups = (behind, here, ahead)
    exists = (
        (me > 0).astype(f32),
        jnp.float32(1.0),
        (me < CORES * zs - 1).astype(f32),
    )
    held = [[groups[q](base + count + w) * exists[q] for w in range(count)] for q in range(3)]
    begin = base_count
    for w in range(count):
        begin -= held[0][w]
    takes = [[] for _ in range(count)]
    for q in range(3):
        for w in range(count):
            end = begin + held[q][w]
            for j in range(count):
                slot = (me * count + j).astype(f32)
                takes[j].append((begin <= slot) & (slot < end))
            begin = end
    coeff = []
    for j in range(count):
        values = []
        for at in range(slots * 2 * nvec):
            slot, rest = divmod(at, 2 * nvec)
            value = jnp.float32(0.0)
            for q in range(3):
                for w in range(count):
                    c = groups[q](slot * per + w * 2 * nvec + rest)
                    value = jnp.where(takes[j][q * count + w], c, value)
            values.append(value)
        coeff.append(values)
        for q in range(3):
            for w in range(count):

                @pl.when(takes[j][q * count + w])
                def _():
                    source[j, :nelec] = walks[q][w, :nelec]
                    source[j, pad : pad + nelec] = walks[q][w, nelec:]

    step = 16
    for side, pieces in enumerate((mine, theirs)):
        at_half = core if side == 0 else CORES - 1 - core
        for p in range(2):

            def add_up(t, _):
                r = pl.multiple_of(t * step, step)
                sums = [jnp.zeros((step, half), f32) for _ in range(2 * count)]
                for k in range(slots):
                    for g in range(nvec):
                        block = pieces[k][p][g, pl.ds(r, step), :]
                        for j in range(count):
                            for ri in range(2):
                                sums[2 * j + ri] += coeff[j][k * 2 * nvec + 2 * g + ri] * block
                for n in range(2 * count):
                    acc[n, at_half, pl.ds(p * part + r, step), :] = sums[n]
                return 0

            lax.fori_loop(0, part // step, add_up, 0)

    i, j_ = ids(half, half)
    for j in range(count):
        for ri in range(2):
            diag = jnp.zeros((1, half), f32)
            for k in range(slots):
                for g in range(nvec):
                    diag += coeff[j][k * 2 * nvec + 2 * g + ri] * smalls[k][g + 1 : g + 2, :]
            square = acc[2 * j + ri, 0]
            turned = square.T
            corner = acc[2 * j + ri, 1]

            def put(value, r, c):
                hi = value.astype(jnp.bfloat16)
                a_hi[j, ri, pl.ds(r, half), pl.ds(c, half)] = hi
                a_lo[j, ri, pl.ds(r, half), pl.ds(c, half)] = (value - hi.astype(f32)).astype(jnp.bfloat16)

            put(jnp.where(i <= j_, square, turned), 0, 0)
            put(jnp.where(i > j_, square, jnp.where(i < j_, turned, diag)), half, half)
            put(corner, 0, half)
            put(corner.T, half, 0)

    for j in range(count):
        for lo in (nelec, pad + nelec):
            source[j, lo : lo + pad - nelec] = jnp.zeros((pad - nelec, norb), f32)
    series = [source[j] for j in range(count)]
    terms = list(series)
    for degree in range(1, TAYLOR + 1):
        for j in range(count):
            term = terms[j]
            hi = term.astype(jnp.bfloat16)
            lo = (term - hi.astype(f32)).astype(jnp.bfloat16)
            both = jnp.concatenate([hi, lo], axis=0)
            prods = []
            for ri in range(2):
                wide = dot(both, a_hi[j, ri])
                prods.append(wide[: 2 * pad] + wide[2 * pad :] + dot(hi, a_lo[j, ri]))
            real = prods[0][:pad] - prods[1][pad:]
            imag = prods[0][pad:] + prods[1][:pad]
            terms[j] = jnp.concatenate([real, imag], axis=0) / degree
            series[j] = series[j] + terms[j]
    for j in range(count):
        out[j, :nelec] = series[j][:nelec]
        out[j, nelec:] = series[j][pad : pad + nelec]


def on_device(walkers, cholesky, fields, weights, counts):
    count, norb, width = walkers.shape
    nvec = cholesky.shape[0]
    half = norb // 2
    part = half // 2
    groups, shards = lax.axis_size("walk"), lax.axis_size("chol")
    zs = groups // CORES
    across = max(d for d in range(1, shards + 1) if shards % d == 0 and d * d <= shards)
    down = shards // across
    me = lax.axis_index("walk").astype(jnp.int32)
    core = me % CORES

    def move(block, dy, dx):
        route = []
        for s in range(shards):
            y, x = divmod(s, across)
            route.append((s, (y + dy) % down * across + (x + dx) % across))
        return lax.ppermute(block, "chol", route)

    def to_core(block):
        return lax.ppermute(block, "walk", [(g, g ^ 1) for g in range(groups)])

    order = [(dy, dx) for dy in range(down) for dx in range(across)]
    own = packed(cholesky, core)
    first, second = own[:, :part], own[:, part:]
    got1, got2 = {(0, 0): first}, {(0, 0): second}
    for dx in range(1, across):
        got1[0, dx] = move(first, 0, dx)
    for dy in range(1, down):
        got2[dy, 0] = move(second, dy, 0)
    for dx in range(1, across):
        got2[0, dx] = move(second, 0, dx)
    for dy in range(1, down):
        got1[dy, 0] = move(first, dy, 0)
    for dy in range(1, down):
        for dx in range(1, across):
            got1[dy, dx] = move(got1[0, dx], dy, 0)
            got2[dy, dx] = move(got2[dy, 0], 0, dx)

    walk_t = jnp.swapaxes(walkers, 1, 2)
    from_behind = lax.ppermute(walk_t, "walk", [(g, g + 1) for g in range(groups - 1)])
    from_ahead = lax.ppermute(walk_t, "walk", [(g + 1, g) for g in range(groups - 1)])

    pad = up_to(width // 2, 128)
    small, other = pl.pallas_call(
        lambda par, fld, wk, vc, sm, ot, fu: prep_kernel(fld, wk, vc, sm, ot, fu, par),
        out_shape=(
            jax.ShapeDtypeStruct((8, half), f32),
            jax.ShapeDtypeStruct((nvec, half, half), f32),
        ),
        in_specs=[SMEM, SMEM, VMEM, VMEM],
        out_specs=(VMEM, VMEM),
        scratch_shapes=[pltpu.VMEM((count, 2 * pad, norb), f32)],
        compiler_params=PARAMS,
        cost_estimate=pl.CostEstimate(flops=5 * 10**9, bytes_accessed=3 * 10**6, transcendentals=0),
    )(core[None], fields, walk_t, cholesky)

    smalls = [small if d == (0, 0) else move(small, *d) for d in order]
    row = pl.pallas_call(
        functools.partial(group_kernel, count, nvec),
        out_shape=jax.ShapeDtypeStruct((1, half), f32),
        in_specs=[SMEM, SMEM] + [VMEM] * shards,
        out_specs=VMEM,
        compiler_params=PARAMS,
    )(weights, counts, *smalls)
    pair = jnp.concatenate([row, to_core(row)], axis=0)
    rows = [pair]
    for k in range(1, zs):
        rows.append(
            lax.ppermute(pair, "walk", [(g, (g + CORES * k) % groups) for g in range(groups)])
        )

    mine = [(got1[d], got2[d]) for d in order]
    theirs = [(other[:, :part], other[:, part:])]
    theirs += [(to_core(got1[d]), to_core(got2[d])) for d in order[1:]]
    flat = [piece for two in mine + theirs for piece in two]
    epad = up_to(width // 2, 16)
    out, marks = pl.pallas_call(
        functools.partial(final_kernel, count, nvec, shards, zs),
        out_shape=(
            jax.ShapeDtypeStruct((count, width, norb), f32),
            jax.ShapeDtypeStruct((1, 128), f32),
        ),
        in_specs=[SMEM] * (1 + zs) + [VMEM] * (3 + shards + len(flat)),
        out_specs=(VMEM, VMEM),
        scratch_shapes=[
            pltpu.VMEM((2 * count, 2, half, half), f32),
            pltpu.VMEM((count, 2, norb, norb), jnp.bfloat16),
            pltpu.VMEM((count, 2, norb, norb), jnp.bfloat16),
            pltpu.VMEM((count, 2 * epad, norb), f32),
        ],
        compiler_params=PARAMS,
        cost_estimate=pl.CostEstimate(flops=10**10, bytes_accessed=10**7, transcendentals=0),
    )(jnp.stack([me, core]), *rows, from_behind, walk_t, from_ahead, *smalls, *flat)
    return jnp.swapaxes(out, 1, 2), marks[0, :count]


def solution(mesh):
    in_specs = (
        P("walk", None, None),
        P("chol", None, None),
        P("walk", "chol"),
        P("walk"),
        P("walk"),
    )
    out_specs = (P("walk", None, None), P("walk"))
    return jax.shard_map(
        on_device, mesh=mesh, in_specs=in_specs, out_specs=out_specs, check_vma=False
    )
```

```python
import functools
import jax
import jax.numpy as jnp
from jax import lax
from jax.experimental import pallas as pl
from jax.experimental.pallas import tpu as pltpu
from jax.sharding import PartitionSpec as P

TAYLOR = 3
NEWTON = 3
CORES = 2
ROOT_DT = 0.1
SMALL = 8
EARLY_COST = 0
K_COST = 0
K2_COST = 4 * 10**9
EDGE_STEP = 0
LATE_COST = 10 * 10**9

f32 = jnp.float32
highest = lax.Precision.HIGHEST
VMEM = pl.BlockSpec(memory_space=pltpu.VMEM)
SMEM = pl.BlockSpec(memory_space=pltpu.SMEM)
HBM = pl.BlockSpec(memory_space=pltpu.HBM)
PARAMS = pltpu.CompilerParams(vmem_limit_bytes=24 * 2**20)


def dot(left, right, precision=None):
    return jnp.dot(left, right, precision=precision, preferred_element_type=f32)


def ids(rows, columns):
    shape = (rows, columns)
    return (
        lax.broadcasted_iota(jnp.int32, shape, 0),
        lax.broadcasted_iota(jnp.int32, shape, 1),
    )


def up_to(n, unit):
    return -(-n // unit) * unit


def pack_kernel(which, vec, first, second, other, top, diags):
    nvec, norb = vec.shape[:2]
    half = norb // 2
    part = half // 2
    rows = top.shape[1]
    i, j = ids(part, half)

    def write(triangles, corners):
        for g in range(nvec):
            for n in range(2):
                rows_in = pl.ds(n * part, part)
                rows_out = pl.ds(g * part, part)
                lower = vec[g, pl.ds(half + n * part, part), half:]
                triangles[n][rows_out] = jnp.where(i + n * part <= j, vec[g, rows_in, :half], lower)
                corners[n][rows_out] = vec[g, rows_in, half:]

    @pl.when(which[1] == 0)
    def _():
        write((first, second), (other.at[0], other.at[1]))

    @pl.when(which[1] != 0)
    def _():
        write((other.at[0], other.at[1]), (first, second))

    diags[...] = jnp.zeros_like(diags)
    i, j = ids(half, half)
    for g in range(nvec):
        top[g] = vec[g, :rows]
        corner = jnp.where(i == j, vec[g, half:, half:], 0.0)
        diags[g + 1 : g + 2] = jnp.sum(corner, axis=0, keepdims=True)


def pack(which, cholesky, rows):
    nvec, norb = cholesky.shape[:2]
    half = norb // 2
    piece = (nvec * half // 2, half)
    return pl.pallas_call(
        pack_kernel,
        out_shape=tuple(
            jax.ShapeDtypeStruct(shape, f32)
            for shape in (piece, piece, (2, *piece), (nvec, rows, norb), (SMALL, half))
        ),
        in_specs=[SMEM, VMEM],
        out_specs=(VMEM,) * 5,
        compiler_params=PARAMS,
        cost_estimate=pl.CostEstimate(flops=10**6, bytes_accessed=4 * 10**6, transcendentals=0),
    )(which, cholesky)


def prep_kernel(fields, walk, tops, diags, small, full):
    count, width, norb = walk.shape
    half = norb // 2
    nelec = width // 2
    pad = up_to(nelec, 128)
    nvec = tops.shape[0]
    i, j = ids(pad, pad)
    twice = jnp.concatenate(
        [jnp.where((i == j) & (i < nelec), 2.0, 0.0), jnp.zeros((pad, pad))], axis=1
    ).astype(f32)
    inside = j < nelec
    full[...] = jnp.zeros_like(full)

    def spread(top):
        return jnp.concatenate(
            [top, jnp.concatenate([-top[:, pad:], top[:, :pad]], axis=1)], axis=0
        )

    inv, over = [], []
    for w in range(count):
        full[w, :nelec] = walk[w, :nelec]
        full[w, pad : pad + nelec] = walk[w, nelec:]
        over_real = jnp.where(inside, full[w, :pad, :pad], 0.0)
        over_imag = jnp.where(inside, full[w, pad:, :pad], 0.0)
        top = jnp.concatenate([over_real, -over_imag], axis=1)
        inv.append(twice - top)
        over.append(spread(top))
    for _ in range(NEWTON - 1):
        left = [twice - dot(inv[w], over[w], highest) for w in range(count)]
        inv = [dot(left[w], spread(inv[w]), highest) for w in range(count)]
    rows = up_to(nelec, 8)
    lane = lax.broadcasted_iota(jnp.int32, (1, half), 1)
    row = jnp.zeros((1, half), f32)
    for w in range(count):
        theta = dot(spread(inv[w]), full[w], highest)
        log_part = jnp.zeros((1, 1), f32)
        for g in range(nvec):
            top = tops[g]
            xr = ROOT_DT * jnp.sum(top * theta[:rows], keepdims=True)
            xi = ROOT_DT * jnp.sum(top * theta[pad : pad + rows], keepdims=True)
            field = fields[w, g]
            at = 2 * (w * nvec + g)
            row += jnp.where(lane == at, ROOT_DT * xi, 0.0)
            row += jnp.where(lane == at + 1, ROOT_DT * (field - xr), 0.0)
            log_part += field * xr - 0.5 * (xr * xr - xi * xi)
        row += jnp.where(lane == 2 * count * nvec + w, log_part, 0.0)
    mask = lax.broadcasted_iota(jnp.int32, (SMALL, half), 0) == 0
    small[...] = jnp.where(mask, row, diags[...])


def group_kernel(count, nvec, weights, counts, *refs):
    smalls, out = refs[:-1], refs[-1]
    width = out.shape[1]
    lane = lax.broadcasted_iota(jnp.int32, (1, width), 1)
    per = 2 * count * nvec
    lines = [s[0:1] for s in smalls]
    logs = lines[0]
    for line in lines[1:]:
        logs = logs + line
    row = jnp.zeros((1, width), f32)
    for k, line in enumerate(lines):
        mine = jnp.where(lane < per, line, 0.0)
        row += mine if k == 0 else pltpu.roll(mine, k * per, 1)
    base = per * len(lines)
    for w in range(count):
        log_weight = jnp.sum(jnp.where(lane == per + w, logs, 0.0), axis=1, keepdims=True)
        row += jnp.where(lane == base + w, weights[w] * jnp.exp(log_weight), 0.0)
        row += jnp.where(lane == base + count + w, counts[w].astype(f32), 0.0)
    out[...] = row


def add_pieces(acc, base, at_half, p, pieces, coeff, part, step):
    def add_up(t, _):
        r = pl.multiple_of(t * step, step)
        here = pl.ds(pl.multiple_of(p * part + r, step), step)
        if base is None:
            sums = [None] * len(coeff)
        else:
            sums = [base[n, at_half, here, :] for n in range(len(coeff))]
        for k, piece in enumerate(pieces):
            for g in range(len(coeff[0][k])):
                block = piece[pl.ds(pl.multiple_of(g * part + r, step), step), :]
                for n in range(len(coeff)):
                    more = coeff[n][k][g] * block
                    sums[n] = more if sums[n] is None else sums[n] + more
        for n in range(len(coeff)):
            acc[n, at_half, here, :] = sums[n]
        return 0

    lax.fori_loop(0, part // step, add_up, 0)


def first_kernel(count, nvec, slots, late, zs, swaps, where_at, rows, *refs):
    refs = list(refs)

    def take(n):
        head = refs[:n]
        del refs[:n]
        return head

    early = slots - len(late)
    walks = take(3)
    smalls = take(slots)
    mine = take(2 * early)
    other, joined = take(2)
    acc, diags, source, marks, late_coeff = refs
    me, core = where_at[0], where_at[1]
    per = 2 * count * nvec
    base = per * slots
    width = walks[0].shape[1]
    nelec = width // 2
    norb = walks[0].shape[2]
    half = norb // 2
    part = half // 2
    pad = source.shape[1] // 2

    def row_of(group):
        return group ^ me if swaps else group

    total = jnp.float32(0.0)
    before = jnp.float32(0.0)
    base_count = jnp.float32(0.0)
    for group in range(CORES * zs):
        at = row_of(jnp.int32(group))
        earlier = (group < me).astype(f32)
        for w in range(count):
            weight = rows[at, base + w]
            total += weight
            before += earlier * weight
            base_count += earlier * rows[at, base + count + w]
    lane = lax.broadcasted_iota(jnp.int32, marks.shape, 1)
    mark_row = jnp.zeros(marks.shape, f32)
    for w in range(count):
        before += rows[row_of(me), base + w]
        mark_row += jnp.where(lane == w, before, 0.0)
    marks[...] = (CORES * zs * count) * mark_row / jnp.full(marks.shape, total, f32)

    lines, held = [], []
    for q in range(3):
        group = me + (q - 1)
        exists = (group >= 0) & (group < CORES * zs)
        lines.append(row_of(jnp.where(exists, group, me)))
        held.append(
            [jnp.where(exists, rows[lines[q], base + count + w], 0.0) for w in range(count)]
        )
    begin = base_count
    for w in range(count):
        begin -= held[0][w]
    line = [jnp.int32(0)] * count
    which = [jnp.int32(0)] * count
    place = [jnp.int32(0)] * count
    for q in range(3):
        at = jnp.int32(0) if q == 1 else jnp.where(core == (1 if q == 0 else 0), 1, 2)
        for w in range(count):
            end = begin + held[q][w]
            for j in range(count):
                slot = (me * count + j).astype(f32)
                chosen = (begin <= slot) & (slot < end)
                line[j] = jnp.where(chosen, lines[q], line[j])
                which[j] = jnp.where(chosen, w, which[j])
                place[j] = jnp.where(chosen, at, place[j])
            begin = end
    coeff = []
    for j in range(count):
        for ri in range(2):
            coeff.append(
                [
                    [
                        rows[line[j], slot * per + which[j] * 2 * nvec + 2 * g + ri]
                        for g in range(nvec)
                    ]
                    for slot in range(slots)
                ]
            )
        for k in range(3):

            @pl.when(place[j] == k)
            def _():
                source[j, :nelec] = walks[k][which[j], :nelec]
                source[j, pad : pad + nelec] = walks[k][which[j], nelec:]

        for lo in (nelec, pad + nelec):
            source[j, lo : lo + pad - nelec] = jnp.zeros((pad - nelec, norb), f32)

    for n in range(2 * count):
        for k, slot in enumerate(late):
            for g in range(nvec):
                late_coeff[n, k * nvec + g] = coeff[n][slot][g]
        diag = jnp.zeros((1, half), f32)
        for k in range(slots):
            for g in range(nvec):
                diag += coeff[n][k][g] * smalls[k][g + 1 : g + 2, :]
        diags[n : n + 1] = diag
    now = [[c[k] for k in range(slots) if k not in late] for c in coeff]
    size = nvec * part
    theirs = [other.at[0], other.at[1]]
    theirs += [joined.at[pl.ds(n * size, size)] for n in range(2 * early - 2)]
    for side, pieces in enumerate((mine, theirs)):
        at_half = core if side == 0 else CORES - 1 - core
        for p in range(2):
            add_pieces(acc, None, at_half, p, pieces[p::2], now, part, 16)


def last_kernel(count, nvec, late, where_at, late_coeff, early, diags, source, *refs):
    pieces, (out, acc, a_hi, a_lo) = list(refs[:-4]), refs[-4:]
    if late:
        joined = pieces.pop()
        size = joined.shape[0] // (2 * late)
        pieces += [joined.at[pl.ds(n * size, size)] for n in range(2 * late)]
    core = where_at[1]
    half = early.shape[2]
    part = half // 2
    pad = source.shape[1] // 2
    nelec = out.shape[1] // 2
    coeff = [
        [[late_coeff[n, k * nvec + g] for g in range(nvec)] for k in range(late)]
        for n in range(2 * count)
    ]
    for side in range(2):
        at_half = core if side == 0 else CORES - 1 - core
        for p in range(2):
            at = 2 * late * side + p
            add_pieces(acc, early, at_half, p, pieces[at : at + 2 * late : 2], coeff, part, 16)

    i, j_ = ids(half, half)
    for j in range(count):
        for ri in range(2):
            diag = diags[2 * j + ri : 2 * j + ri + 1]
            square = acc[2 * j + ri, 0]
            turned = square.T
            corner = acc[2 * j + ri, 1]

            def put(value, r, c):
                hi = value.astype(jnp.bfloat16)
                a_hi[j, ri, pl.ds(r, half), pl.ds(c, half)] = hi
                a_lo[j, ri, pl.ds(r, half), pl.ds(c, half)] = (value - hi.astype(f32)).astype(jnp.bfloat16)

            put(jnp.where(i <= j_, square, turned), 0, 0)
            put(jnp.where(i > j_, square, jnp.where(i < j_, turned, diag)), half, half)
            put(corner, 0, half)
            put(corner.T, half, 0)

    series = [source[j] for j in range(count)]
    terms = list(series)
    for degree in range(1, TAYLOR + 1):
        for j in range(count):
            term = terms[j]
            hi = term.astype(jnp.bfloat16)
            lo = (term - hi.astype(f32)).astype(jnp.bfloat16)
            both = jnp.concatenate([hi, lo], axis=0)
            prods = []
            for ri in range(2):
                wide = dot(both, a_hi[j, ri])
                prods.append(wide[: 2 * pad] + wide[2 * pad :] + dot(hi, a_lo[j, ri]))
            real = prods[0][:pad] - prods[1][pad:]
            imag = prods[0][pad:] + prods[1][:pad]
            terms[j] = jnp.concatenate([real, imag], axis=0) / degree
            series[j] = series[j] + terms[j]
    for j in range(count):
        out[j, :nelec] = series[j][:nelec]
        out[j, nelec:] = series[j][pad : pad + nelec]


def join_kernel(*refs):
    size = refs[0].shape[0]
    for n, ref in enumerate(refs[:-1]):
        refs[-1][n * size : (n + 1) * size] = ref[...]


def join(pieces, cost):
    rows, columns = pieces[0].shape
    return pl.pallas_call(
        join_kernel,
        out_shape=jax.ShapeDtypeStruct((len(pieces) * rows, columns), f32),
        in_specs=[VMEM] * len(pieces),
        out_specs=VMEM,
        compiler_params=PARAMS,
        cost_estimate=pl.CostEstimate(flops=cost, bytes_accessed=10, transcendentals=0),
    )(*pieces)


def after(value, *others):
    return lax.optimization_barrier((value, *others))[0]


def on_device(walkers, cholesky, fields, weights, counts):
    count, norb, width = walkers.shape
    nvec = cholesky.shape[0]
    half = norb // 2
    part = half // 2
    groups, shards = lax.axis_size("walk"), lax.axis_size("chol")
    zs = groups // CORES
    across = max(d for d in range(1, shards + 1) if shards % d == 0 and d * d <= shards)
    down = shards // across
    me = lax.axis_index("walk").astype(jnp.int32)
    core = me % CORES
    where_at = jnp.stack([me, core])

    def move(block, dy, dx):
        route = []
        for s in range(shards):
            y, x = divmod(s, across)
            route.append((s, (y + dy) % down * across + (x + dx) % across))
        return lax.ppermute(block, "chol", route)

    def to_core(block):
        return lax.ppermute(block, "walk", [(g, g ^ 1) for g in range(groups)])

    def over_edge(block):
        route = [(g, g + 1) for g in range(1, groups - 1, CORES)]
        return lax.ppermute(block, "walk", route + [(b, a) for a, b in route])

    order = [(dy, dx) for dy in range(down) for dx in range(across)]
    late = [k for k, (dy, dx) in enumerate(order) if dy and dx]
    walk_t = jnp.swapaxes(walkers, 1, 2)

    first, second, other, top, diags = pack(where_at, cholesky, up_to(width // 2, 8))
    got1, got2 = {(0, 0): first}, {(0, 0): second}
    for dx in range(1, across):
        got1[0, dx] = move(first, 0, dx)
    for dy in range(1, down):
        got2[dy, 0] = move(second, dy, 0)

    edge_walk = over_edge(after(walk_t, first))

    pad = up_to(width // 2, 128)
    small = pl.pallas_call(
        prep_kernel,
        out_shape=jax.ShapeDtypeStruct((SMALL, half), f32),
        in_specs=[SMEM] + [VMEM] * 3,
        out_specs=VMEM,
        scratch_shapes=[pltpu.VMEM((count, 2 * pad, norb), f32)],
        compiler_params=PARAMS,
        cost_estimate=pl.CostEstimate(flops=10**10, bytes_accessed=3 * 10**6, transcendentals=0),
    )(fields, walk_t, top, diags)
    smalls = [small if d == (0, 0) else move(small, *d) for d in order]
    for dx in range(1, across):
        got2[0, dx] = move(after(second, small, got1[0, dx]), 0, dx)
    for dy in range(1, down):
        got1[dy, 0] = move(after(first, small, got2[dy, 0]), dy, 0)
    for dy in range(1, down):
        for dx in range(1, across):
            got1[dy, dx] = move(got1[0, dx], dy, 0)
            got2[dy, dx] = move(got2[dy, 0], 0, dx)

    mine = [(got1[d], got2[d]) for d in order]
    joint = [p for k, two in enumerate(mine) for p in two if k and k not in late]
    core_walk = to_core(after(walk_t, small))
    row = pl.pallas_call(
        functools.partial(group_kernel, count, nvec),
        out_shape=jax.ShapeDtypeStruct((1, half), f32),
        in_specs=[SMEM, SMEM] + [VMEM] * shards,
        out_specs=VMEM,
        compiler_params=PARAMS,
        cost_estimate=pl.CostEstimate(flops=K2_COST, bytes_accessed=10, transcendentals=0),
    )(weights, counts, *smalls)
    swaps = groups & (groups - 1) == 0
    if swaps:
        rows = row
        for k in range(groups.bit_length() - 1):
            route = [(g, g ^ 2**k) for g in range(groups)]
            if k == EDGE_STEP:
                rows = after(rows, edge_walk)
            rows = jnp.concatenate([rows, lax.ppermute(rows, "walk", route)], axis=0)
            pair = rows if k < 2 else pair
    else:
        rows = pair = lax.all_gather(row, "walk", axis=0, tiled=True)
    joined = to_core(join([after(p, pair) for p in joint], EARLY_COST))
    my_late = [p for k in late for p in mine[k]]
    their_late = to_core(join(my_late, LATE_COST)) if late else None
    soon = [p for k, two in enumerate(mine) for p in two if k not in late] + [other, joined]
    epad = up_to(width // 2, 16)
    acc, diags, source, marks, late_coeff = pl.pallas_call(
        functools.partial(first_kernel, count, nvec, shards, late, zs, swaps),
        out_shape=(
            jax.ShapeDtypeStruct((2 * count, 2, half, half), f32),
            jax.ShapeDtypeStruct((up_to(2 * count, 8), half), f32),
            jax.ShapeDtypeStruct((count, 2 * epad, norb), f32),
            jax.ShapeDtypeStruct((1, 128), f32),
            jax.ShapeDtypeStruct((2 * count, max(1, len(late)) * nvec), f32),
        ),
        in_specs=[SMEM] * 2 + [VMEM] * (3 + shards + len(soon)),
        out_specs=(VMEM, VMEM, VMEM, VMEM, SMEM),
        compiler_params=PARAMS,
        cost_estimate=pl.CostEstimate(flops=K_COST, bytes_accessed=10, transcendentals=0),
    )(where_at, rows, walk_t, core_walk, edge_walk, *smalls, *soon)

    rest = my_late + ([their_late] if late else [])
    out = pl.pallas_call(
        functools.partial(last_kernel, count, nvec, len(late)),
        out_shape=jax.ShapeDtypeStruct((count, width, norb), f32),
        in_specs=[SMEM, SMEM] + [VMEM] * (3 + len(rest)),
        out_specs=VMEM,
        scratch_shapes=[
            pltpu.VMEM((2 * count, 2, half, half), f32),
            pltpu.VMEM((count, 2, norb, norb), jnp.bfloat16),
            pltpu.VMEM((count, 2, norb, norb), jnp.bfloat16),
        ],
        compiler_params=PARAMS,
        cost_estimate=pl.CostEstimate(flops=10**10, bytes_accessed=10**7, transcendentals=0),
    )(where_at, late_coeff, acc, diags, source, *rest)
    return jnp.swapaxes(out, 1, 2), marks[0, :count]


def solution(mesh):
    in_specs = (
        P("walk", None, None),
        P("chol", None, None),
        P("walk", "chol"),
        P("walk"),
        P("walk"),
    )
    out_specs = (P("walk", None, None), P("walk"))
    return jax.shard_map(
        on_device, mesh=mesh, in_specs=in_specs, out_specs=out_specs, check_vma=False
    )
```

```python
import functools
import jax
import jax.numpy as jnp
from jax import lax
from jax.experimental import pallas as pl
from jax.experimental.pallas import tpu as pltpu
from jax.sharding import PartitionSpec as P

TAYLOR = 3
NEWTON = 3
CORES = 2
ROOT_DT = 0.1
SMALL = 8
EARLY_COST = 0
K_COST = 0
K2_COST = 4 * 10**9
EDGE_STEP = 0
LATE_COST = 10 * 10**9

f32 = jnp.float32
highest = lax.Precision.HIGHEST
VMEM = pl.BlockSpec(memory_space=pltpu.VMEM)
SMEM = pl.BlockSpec(memory_space=pltpu.SMEM)
HBM = pl.BlockSpec(memory_space=pltpu.HBM)
PARAMS = pltpu.CompilerParams(vmem_limit_bytes=24 * 2**20)


def dot(left, right, precision=None):
    return jnp.dot(left, right, precision=precision, preferred_element_type=f32)


def ids(rows, columns):
    shape = (rows, columns)
    return (
        lax.broadcasted_iota(jnp.int32, shape, 0),
        lax.broadcasted_iota(jnp.int32, shape, 1),
    )


def up_to(n, unit):
    return -(-n // unit) * unit


def pack_kernel(which, vec, first, second, other, top, diags):
    nvec, norb = vec.shape[:2]
    half = norb // 2
    part = half // 2
    rows = top.shape[1]
    i, j = ids(part, half)

    def write(triangles, corners):
        for g in range(nvec):
            for n in range(2):
                rows_in = pl.ds(n * part, part)
                rows_out = pl.ds(g * part, part)
                lower = vec[g, pl.ds(half + n * part, part), half:]
                triangles[n][rows_out] = jnp.where(i + n * part <= j, vec[g, rows_in, :half], lower)
                corners[n][rows_out] = vec[g, rows_in, half:]

    @pl.when(which[1] == 0)
    def _():
        write((first, second), (other.at[0], other.at[1]))

    @pl.when(which[1] != 0)
    def _():
        write((other.at[0], other.at[1]), (first, second))

    diags[...] = jnp.zeros_like(diags)
    i, j = ids(half, half)
    for g in range(nvec):
        top[g] = vec[g, :rows]
        corner = jnp.where(i == j, vec[g, half:, half:], 0.0)
        diags[g + 1 : g + 2] = jnp.sum(corner, axis=0, keepdims=True)


def pack(which, cholesky, rows):
    nvec, norb = cholesky.shape[:2]
    half = norb // 2
    piece = (nvec * half // 2, half)
    return pl.pallas_call(
        pack_kernel,
        out_shape=tuple(
            jax.ShapeDtypeStruct(shape, f32)
            for shape in (piece, piece, (2, *piece), (nvec, rows, norb), (SMALL, half))
        ),
        in_specs=[SMEM, VMEM],
        out_specs=(VMEM,) * 5,
        compiler_params=PARAMS,
        cost_estimate=pl.CostEstimate(flops=10**6, bytes_accessed=4 * 10**6, transcendentals=0),
    )(which, cholesky)


def prep_kernel(fields, walk, tops, diags, small, full):
    count, width, norb = walk.shape
    half = norb // 2
    nelec = width // 2
    pad = up_to(nelec, 128)
    nvec = tops.shape[0]
    i, j = ids(pad, pad)
    twice = jnp.concatenate(
        [jnp.where((i == j) & (i < nelec), 2.0, 0.0), jnp.zeros((pad, pad))], axis=1
    ).astype(f32)
    inside = j < nelec
    full[...] = jnp.zeros_like(full)

    def spread(top):
        return jnp.concatenate(
            [top, jnp.concatenate([-top[:, pad:], top[:, :pad]], axis=1)], axis=0
        )

    inv, over = [], []
    for w in range(count):
        full[w, :nelec] = walk[w, :nelec]
        full[w, pad : pad + nelec] = walk[w, nelec:]
        over_real = jnp.where(inside, full[w, :pad, :pad], 0.0)
        over_imag = jnp.where(inside, full[w, pad:, :pad], 0.0)
        top = jnp.concatenate([over_real, -over_imag], axis=1)
        inv.append(twice - top)
        over.append(spread(top))
    for _ in range(NEWTON - 1):
        left = [twice - dot(inv[w], over[w], highest) for w in range(count)]
        inv = [dot(left[w], spread(inv[w]), highest) for w in range(count)]
    rows = up_to(nelec, 8)
    lane = lax.broadcasted_iota(jnp.int32, (1, half), 1)
    row = jnp.zeros((1, half), f32)
    for w in range(count):
        theta = dot(spread(inv[w]), full[w], highest)
        log_part = jnp.zeros((1, 1), f32)
        for g in range(nvec):
            top = tops[g]
            xr = ROOT_DT * jnp.sum(top * theta[:rows], keepdims=True)
            xi = ROOT_DT * jnp.sum(top * theta[pad : pad + rows], keepdims=True)
            field = fields[w, g]
            at = 2 * (w * nvec + g)
            row += jnp.where(lane == at, ROOT_DT * xi, 0.0)
            row += jnp.where(lane == at + 1, ROOT_DT * (field - xr), 0.0)
            log_part += field * xr - 0.5 * (xr * xr - xi * xi)
        row += jnp.where(lane == 2 * count * nvec + w, log_part, 0.0)
    mask = lax.broadcasted_iota(jnp.int32, (SMALL, half), 0) == 0
    small[...] = jnp.where(mask, row, diags[...])


def group_kernel(count, nvec, weights, counts, *refs):
    smalls, out = refs[:-1], refs[-1]
    width = out.shape[1]
    lane = lax.broadcasted_iota(jnp.int32, (1, width), 1)
    per = 2 * count * nvec
    lines = [s[0:1] for s in smalls]
    logs = lines[0]
    for line in lines[1:]:
        logs = logs + line
    row = jnp.zeros((1, width), f32)
    for k, line in enumerate(lines):
        mine = jnp.where(lane < per, line, 0.0)
        row += mine if k == 0 else pltpu.roll(mine, k * per, 1)
    base = per * len(lines)
    for w in range(count):
        log_weight = jnp.sum(jnp.where(lane == per + w, logs, 0.0), axis=1, keepdims=True)
        row += jnp.where(lane == base + w, weights[w] * jnp.exp(log_weight), 0.0)
        row += jnp.where(lane == base + count + w, counts[w].astype(f32), 0.0)
    out[...] = row


def add_pieces(acc, base, at_half, p, pieces, coeff, part, step):
    def add_up(t, _):
        r = pl.multiple_of(t * step, step)
        here = pl.ds(pl.multiple_of(p * part + r, step), step)
        if base is None:
            sums = [None] * len(coeff)
        else:
            sums = [base[n, at_half, here, :] for n in range(len(coeff))]
        for k, piece in enumerate(pieces):
            for g in range(len(coeff[0][k])):
                block = piece[pl.ds(pl.multiple_of(g * part + r, step), step), :]
                for n in range(len(coeff)):
                    more = coeff[n][k][g] * block
                    sums[n] = more if sums[n] is None else sums[n] + more
        for n in range(len(coeff)):
            acc[n, at_half, here, :] = sums[n]
        return 0

    lax.fori_loop(0, part // step, add_up, 0)


def first_kernel(count, nvec, slots, late, zs, swaps, where_at, rows, *refs):
    refs = list(refs)

    def take(n):
        head = refs[:n]
        del refs[:n]
        return head

    early = slots - len(late)
    walks = take(3)
    smalls = take(slots)
    mine = take(2 * early)
    other, joined = take(2)
    acc, diags, source, marks, late_coeff = refs
    me, core = where_at[0], where_at[1]
    per = 2 * count * nvec
    base = per * slots
    width = walks[0].shape[1]
    nelec = width // 2
    norb = walks[0].shape[2]
    half = norb // 2
    part = half // 2
    pad = source.shape[1] // 2

    def row_of(group):
        return group ^ me if swaps else group

    total = jnp.float32(0.0)
    before = jnp.float32(0.0)
    base_count = jnp.float32(0.0)
    for group in range(CORES * zs):
        at = row_of(jnp.int32(group))
        earlier = (group < me).astype(f32)
        for w in range(count):
            weight = rows[at, base + w]
            total += weight
            before += earlier * weight
            base_count += earlier * rows[at, base + count + w]
    for w in range(count):
        before += rows[row_of(me), base + w]
        marks[w] = (CORES * zs * count) * before / total

    lines, held = [], []
    for q in range(3):
        group = me + (q - 1)
        exists = (group >= 0) & (group < CORES * zs)
        lines.append(row_of(jnp.where(exists, group, me)))
        held.append(
            [jnp.where(exists, rows[lines[q], base + count + w], 0.0) for w in range(count)]
        )
    begin = base_count
    for w in range(count):
        begin -= held[0][w]
    line = [jnp.int32(0)] * count
    which = [jnp.int32(0)] * count
    place = [jnp.int32(0)] * count
    for q in range(3):
        at = jnp.int32(0) if q == 1 else jnp.where(core == (1 if q == 0 else 0), 1, 2)
        for w in range(count):
            end = begin + held[q][w]
            for j in range(count):
                slot = (me * count + j).astype(f32)
                chosen = (begin <= slot) & (slot < end)
                line[j] = jnp.where(chosen, lines[q], line[j])
                which[j] = jnp.where(chosen, w, which[j])
                place[j] = jnp.where(chosen, at, place[j])
            begin = end
    coeff = []
    for j in range(count):
        for ri in range(2):
            coeff.append(
                [
                    [
                        rows[line[j], slot * per + which[j] * 2 * nvec + 2 * g + ri]
                        for g in range(nvec)
                    ]
                    for slot in range(slots)
                ]
            )
        for k in range(3):

            @pl.when(place[j] == k)
            def _():
                source[j, :nelec] = walks[k][which[j], :nelec]
                source[j, pad : pad + nelec] = walks[k][which[j], nelec:]

        for lo in (nelec, pad + nelec):
            source[j, lo : lo + pad - nelec] = jnp.zeros((pad - nelec, norb), f32)

    for n in range(2 * count):
        for k, slot in enumerate(late):
            for g in range(nvec):
                late_coeff[n, k * nvec + g] = coeff[n][slot][g]
        diag = jnp.zeros((1, half), f32)
        for k in range(slots):
            for g in range(nvec):
                diag += coeff[n][k][g] * smalls[k][g + 1 : g + 2, :]
        diags[n : n + 1] = diag
    now = [[c[k] for k in range(slots) if k not in late] for c in coeff]
    size = nvec * part
    theirs = [other.at[0], other.at[1]]
    theirs += [joined.at[pl.ds(n * size, size)] for n in range(2 * early - 2)]
    for side, pieces in enumerate((mine, theirs)):
        at_half = core if side == 0 else CORES - 1 - core
        for p in range(2):
            add_pieces(acc, None, at_half, p, pieces[p::2], now, part, 16)


def last_kernel(count, nvec, late, where_at, late_coeff, early, diags, source, *refs):
    pieces, (out, acc, a_hi, a_lo) = list(refs[:-4]), refs[-4:]
    if late:
        joined = pieces.pop()
        size = joined.shape[0] // (2 * late)
        pieces += [joined.at[pl.ds(n * size, size)] for n in range(2 * late)]
    core = where_at[1]
    half = early.shape[2]
    part = half // 2
    pad = source.shape[1] // 2
    nelec = out.shape[1] // 2
    coeff = [
        [[late_coeff[n, k * nvec + g] for g in range(nvec)] for k in range(late)]
        for n in range(2 * count)
    ]
    for side in range(2):
        at_half = core if side == 0 else CORES - 1 - core
        for p in range(2):
            at = 2 * late * side + p
            add_pieces(acc, early, at_half, p, pieces[at : at + 2 * late : 2], coeff, part, 16)

    i, j_ = ids(half, half)

    def unpack(j):
        blocks = []
        for ri in range(2):
            diag = diags[2 * j + ri : 2 * j + ri + 1]
            square = acc[2 * j + ri, 0]
            turned = square.T
            corner = acc[2 * j + ri, 1]
            blocks.append(
                (
                    jnp.where(i <= j_, square, turned),
                    corner,
                    corner.T,
                    jnp.where(i > j_, square, jnp.where(i < j_, turned, diag)),
                )
            )
        for n in range(4):
            re, im = blocks[0][n], blocks[1][n]
            r, c = half * (n // 2), half * (n % 2)
            for k, value in enumerate((re, im - re, im + re)):
                hi = value.astype(jnp.bfloat16)
                a_hi[j, k, r : r + half, c : c + half] = hi
                a_lo[j, k, r : r + half, c : c + half] = (value - hi.astype(f32)).astype(jnp.bfloat16)

    terms = [source[j] for j in range(count)]
    series = list(terms)

    def advance(j, degree):
        term = terms[j]
        prods = []
        for n, left in enumerate((term[:pad] + term[pad:], term[:pad], term[pad:])):
            hi = left.astype(jnp.bfloat16)
            lo = (left - hi.astype(f32)).astype(jnp.bfloat16)
            wide = dot(jnp.concatenate([hi, lo], axis=0), a_hi[j, n])
            prods.append(wide[:pad] + wide[pad:] + dot(hi, a_lo[j, n]))
        terms[j] = jnp.concatenate([prods[0] - prods[2], prods[0] + prods[1]], axis=0) / degree
        series[j] = series[j] + terms[j]

    for j in range(count):
        unpack(j)
    for degree in range(1, TAYLOR + 1):
        for j in range(count):
            advance(j, degree)
    for j in range(count):
        out[j, :nelec] = series[j][:nelec]
        out[j, nelec:] = series[j][pad : pad + nelec]


def join_kernel(*refs):
    size = refs[0].shape[0]
    for n, ref in enumerate(refs[:-1]):
        refs[-1][n * size : (n + 1) * size] = ref[...]


def join(pieces, cost):
    rows, columns = pieces[0].shape
    return pl.pallas_call(
        join_kernel,
        out_shape=jax.ShapeDtypeStruct((len(pieces) * rows, columns), f32),
        in_specs=[VMEM] * len(pieces),
        out_specs=VMEM,
        compiler_params=PARAMS,
        cost_estimate=pl.CostEstimate(flops=cost, bytes_accessed=10, transcendentals=0),
    )(*pieces)


def after(value, *others):
    return lax.optimization_barrier((value, *others))[0]


def on_device(walkers, cholesky, fields, weights, counts):
    count, norb, width = walkers.shape
    nvec = cholesky.shape[0]
    half = norb // 2
    part = half // 2
    groups, shards = lax.axis_size("walk"), lax.axis_size("chol")
    zs = groups // CORES
    across = max(d for d in range(1, shards + 1) if shards % d == 0 and d * d <= shards)
    down = shards // across
    me = lax.axis_index("walk").astype(jnp.int32)
    core = me % CORES
    where_at = jnp.stack([me, core])

    def move(block, dy, dx):
        route = []
        for s in range(shards):
            y, x = divmod(s, across)
            route.append((s, (y + dy) % down * across + (x + dx) % across))
        return lax.ppermute(block, "chol", route)

    def to_core(block):
        return lax.ppermute(block, "walk", [(g, g ^ 1) for g in range(groups)])

    def over_edge(block):
        route = [(g, g + 1) for g in range(1, groups - 1, CORES)]
        ends = [(g, g) for g in (0, groups - 1)]
        return lax.ppermute(block, "walk", route + [(b, a) for a, b in route] + ends)

    order = [(dy, dx) for dy in range(down) for dx in range(across)]
    late = [k for k, (dy, dx) in enumerate(order) if dy and dx]
    walk_t = jnp.swapaxes(walkers, 1, 2)

    first, second, other, top, diags = pack(where_at, cholesky, up_to(width // 2, 8))
    got1, got2 = {(0, 0): first}, {(0, 0): second}
    for dx in range(1, across):
        got1[0, dx] = move(first, 0, dx)
    for dy in range(1, down):
        got2[dy, 0] = move(second, dy, 0)

    edge_walk = over_edge(after(walk_t, first))

    pad = up_to(width // 2, 128)
    small = pl.pallas_call(
        prep_kernel,
        out_shape=jax.ShapeDtypeStruct((SMALL, half), f32),
        in_specs=[SMEM] + [VMEM] * 3,
        out_specs=VMEM,
        scratch_shapes=[pltpu.VMEM((count, 2 * pad, norb), f32)],
        compiler_params=PARAMS,
        cost_estimate=pl.CostEstimate(flops=10**10, bytes_accessed=3 * 10**6, transcendentals=0),
    )(fields, walk_t, top, diags)
    smalls = [small if d == (0, 0) else move(small, *d) for d in order]
    for dx in range(1, across):
        got2[0, dx] = move(after(second, small, got1[0, dx]), 0, dx)
    for dy in range(1, down):
        got1[dy, 0] = move(after(first, small, got2[dy, 0]), dy, 0)
    for dy in range(1, down):
        for dx in range(1, across):
            got1[dy, dx] = move(got1[0, dx], dy, 0)
            got2[dy, dx] = move(got2[dy, 0], 0, dx)

    mine = [(got1[d], got2[d]) for d in order]
    joint = [p for k, two in enumerate(mine) for p in two if k and k not in late]
    core_walk = to_core(after(walk_t, small))
    row = pl.pallas_call(
        functools.partial(group_kernel, count, nvec),
        out_shape=jax.ShapeDtypeStruct((1, half), f32),
        in_specs=[SMEM, SMEM] + [VMEM] * shards,
        out_specs=VMEM,
        compiler_params=PARAMS,
        cost_estimate=pl.CostEstimate(flops=K2_COST, bytes_accessed=10, transcendentals=0),
    )(weights, counts, *smalls)
    swaps = groups & (groups - 1) == 0
    if swaps:
        rows = row
        for k in range(groups.bit_length() - 1):
            route = [(g, g ^ 2**k) for g in range(groups)]
            if k == EDGE_STEP:
                rows = after(rows, edge_walk)
            rows = jnp.concatenate([rows, lax.ppermute(rows, "walk", route)], axis=0)
            pair = rows if k < 2 else pair
    else:
        rows = pair = lax.all_gather(row, "walk", axis=0, tiled=True)
    joined = to_core(join([after(p, pair) for p in joint], EARLY_COST))
    my_late = [p for k in late for p in mine[k]]
    their_late = to_core(join([after(p, rows) for p in my_late], LATE_COST)) if late else None
    soon = [p for k, two in enumerate(mine) for p in two if k not in late] + [other, joined]
    epad = up_to(width // 2, 16)
    acc, diags, source, marks, late_coeff = pl.pallas_call(
        functools.partial(first_kernel, count, nvec, shards, late, zs, swaps),
        out_shape=(
            jax.ShapeDtypeStruct((2 * count, 2, half, half), f32),
            jax.ShapeDtypeStruct((up_to(2 * count, 8), half), f32),
            jax.ShapeDtypeStruct((count, 2 * epad, norb), f32),
            jax.ShapeDtypeStruct((count,), f32),
            jax.ShapeDtypeStruct((2 * count, max(1, len(late)) * nvec), f32),
        ),
        in_specs=[SMEM] * 2 + [VMEM] * (3 + shards + len(soon)),
        out_specs=(VMEM, VMEM, VMEM, SMEM, SMEM),
        compiler_params=PARAMS,
        cost_estimate=pl.CostEstimate(flops=K_COST, bytes_accessed=10, transcendentals=0),
    )(where_at, rows, walk_t, core_walk, edge_walk, *smalls, *soon)

    rest = my_late + ([their_late] if late else [])
    out = pl.pallas_call(
        functools.partial(last_kernel, count, nvec, len(late)),
        out_shape=jax.ShapeDtypeStruct((count, width, norb), f32),
        in_specs=[SMEM, SMEM] + [VMEM] * (3 + len(rest)),
        out_specs=VMEM,
        scratch_shapes=[
            pltpu.VMEM((2 * count, 2, half, half), f32),
            pltpu.VMEM((count, 3, norb, norb), jnp.bfloat16),
            pltpu.VMEM((count, 3, norb, norb), jnp.bfloat16),
        ],
        compiler_params=PARAMS,
        cost_estimate=pl.CostEstimate(flops=10**10, bytes_accessed=10**7, transcendentals=0),
    )(where_at, late_coeff, acc, diags, source, *rest)
    return jnp.swapaxes(out, 1, 2), marks


def solution(mesh):
    in_specs = (
        P("walk", None, None),
        P("chol", None, None),
        P("walk", "chol"),
        P("walk"),
        P("walk"),
    )
    out_specs = (P("walk", None, None), P("walk"))
    return jax.shard_map(
        on_device, mesh=mesh, in_specs=in_specs, out_specs=out_specs, check_vma=False
    )
```

```python
import functools
import jax
import jax.numpy as jnp
from jax import lax
from jax.experimental import pallas as pl
from jax.experimental.pallas import tpu as pltpu
from jax.sharding import PartitionSpec as P

TAYLOR = 3
NEWTON = 3
CORES = 2
ROOT_DT = 0.1
SMALL = 8
EARLY_COST = 0
K_COST = 0
K2_COST = 4 * 10**9
EDGE_STEP = 0
LATE_COST = 10 * 10**9

f32 = jnp.float32
highest = lax.Precision.HIGHEST
VMEM = pl.BlockSpec(memory_space=pltpu.VMEM)
SMEM = pl.BlockSpec(memory_space=pltpu.SMEM)
HBM = pl.BlockSpec(memory_space=pltpu.HBM)
PARAMS = pltpu.CompilerParams(vmem_limit_bytes=24 * 2**20)


def dot(left, right, precision=None):
    return jnp.dot(left, right, precision=precision, preferred_element_type=f32)


def ids(rows, columns):
    shape = (rows, columns)
    return (
        lax.broadcasted_iota(jnp.int32, shape, 0),
        lax.broadcasted_iota(jnp.int32, shape, 1),
    )


def up_to(n, unit):
    return -(-n // unit) * unit


def pack_kernel(which, vec, first, second, other, top, diags):
    nvec, norb = vec.shape[:2]
    half = norb // 2
    part = half // 2
    rows = top.shape[1]
    i, j = ids(part, half)

    def write(triangles, corners):
        for g in range(nvec):
            for n in range(2):
                rows_in = pl.ds(n * part, part)
                rows_out = pl.ds(g * part, part)
                lower = vec[g, pl.ds(half + n * part, part), half:]
                triangles[n][rows_out] = jnp.where(i + n * part <= j, vec[g, rows_in, :half], lower)
                corners[n][rows_out] = vec[g, rows_in, half:]

    @pl.when(which[1] == 0)
    def _():
        write((first, second), (other.at[0], other.at[1]))

    @pl.when(which[1] != 0)
    def _():
        write((other.at[0], other.at[1]), (first, second))

    diags[...] = jnp.zeros_like(diags)
    i, j = ids(half, half)
    for g in range(nvec):
        top[g] = vec[g, :rows]
        corner = jnp.where(i == j, vec[g, half:, half:], 0.0)
        diags[g + 1 : g + 2] = jnp.sum(corner, axis=0, keepdims=True)


def pack(which, cholesky, rows):
    nvec, norb = cholesky.shape[:2]
    half = norb // 2
    piece = (nvec * half // 2, half)
    return pl.pallas_call(
        pack_kernel,
        out_shape=tuple(
            jax.ShapeDtypeStruct(shape, f32)
            for shape in (piece, piece, (2, *piece), (nvec, rows, norb), (SMALL, half))
        ),
        in_specs=[SMEM, VMEM],
        out_specs=(VMEM,) * 5,
        compiler_params=PARAMS,
        cost_estimate=pl.CostEstimate(flops=10**6, bytes_accessed=4 * 10**6, transcendentals=0),
    )(which, cholesky)


def prep_kernel(fields, walk, tops, diags, small, full):
    count, width, norb = walk.shape
    half = norb // 2
    nelec = width // 2
    pad = up_to(nelec, 128)
    nvec = tops.shape[0]
    i, j = ids(pad, pad)
    twice = jnp.concatenate(
        [jnp.where((i == j) & (i < nelec), 2.0, 0.0), jnp.zeros((pad, pad))], axis=1
    ).astype(f32)
    inside = j < nelec
    full[...] = jnp.zeros_like(full)

    def spread(top):
        return jnp.concatenate(
            [top, jnp.concatenate([-top[:, pad:], top[:, :pad]], axis=1)], axis=0
        )

    inv, over = [], []
    for w in range(count):
        full[w, :nelec] = walk[w, :nelec]
        full[w, pad : pad + nelec] = walk[w, nelec:]
        over_real = jnp.where(inside, full[w, :pad, :pad], 0.0)
        over_imag = jnp.where(inside, full[w, pad:, :pad], 0.0)
        top = jnp.concatenate([over_real, -over_imag], axis=1)
        inv.append(twice - top)
        over.append(spread(top))
    for _ in range(NEWTON - 1):
        left = [twice - dot(inv[w], over[w], highest) for w in range(count)]
        inv = [dot(left[w], spread(inv[w]), highest) for w in range(count)]
    rows = up_to(nelec, 8)
    lane = lax.broadcasted_iota(jnp.int32, (1, half), 1)
    row = jnp.zeros((1, half), f32)
    for w in range(count):
        theta = dot(spread(inv[w]), full[w], highest)
        log_part = jnp.zeros((1, 1), f32)
        for g in range(nvec):
            top = tops[g]
            xr = ROOT_DT * jnp.sum(top * theta[:rows], keepdims=True)
            xi = ROOT_DT * jnp.sum(top * theta[pad : pad + rows], keepdims=True)
            field = fields[w, g]
            at = 2 * (w * nvec + g)
            row += jnp.where(lane == at, ROOT_DT * xi, 0.0)
            row += jnp.where(lane == at + 1, ROOT_DT * (field - xr), 0.0)
            log_part += field * xr - 0.5 * (xr * xr - xi * xi)
        row += jnp.where(lane == 2 * count * nvec + w, log_part, 0.0)
    mask = lax.broadcasted_iota(jnp.int32, (SMALL, half), 0) == 0
    small[...] = jnp.where(mask, row, diags[...])


def group_kernel(count, nvec, weights, counts, *refs):
    smalls, out = refs[:-1], refs[-1]
    width = out.shape[1]
    lane = lax.broadcasted_iota(jnp.int32, (1, width), 1)
    per = 2 * count * nvec
    lines = [s[0:1] for s in smalls]
    logs = lines[0]
    for line in lines[1:]:
        logs = logs + line
    row = jnp.zeros((1, width), f32)
    for k, line in enumerate(lines):
        mine = jnp.where(lane < per, line, 0.0)
        row += mine if k == 0 else pltpu.roll(mine, k * per, 1)
    base = per * len(lines)
    for w in range(count):
        log_weight = jnp.sum(jnp.where(lane == per + w, logs, 0.0), axis=1, keepdims=True)
        row += jnp.where(lane == base + w, weights[w] * jnp.exp(log_weight), 0.0)
        row += jnp.where(lane == base + count + w, counts[w].astype(f32), 0.0)
    out[...] = row


def add_pieces(acc, base, at_half, p, pieces, coeff, part, step):
    def add_up(t, _):
        r = pl.multiple_of(t * step, step)
        here = pl.ds(pl.multiple_of(p * part + r, step), step)
        if base is None:
            sums = [None] * len(coeff)
        else:
            sums = [base[n, at_half, here, :] for n in range(len(coeff))]
        for k, piece in enumerate(pieces):
            for g in range(len(coeff[0][k])):
                block = piece[pl.ds(pl.multiple_of(g * part + r, step), step), :]
                for n in range(len(coeff)):
                    more = coeff[n][k][g] * block
                    sums[n] = more if sums[n] is None else sums[n] + more
        for n in range(len(coeff)):
            acc[n, at_half, here, :] = sums[n]
        return 0

    lax.fori_loop(0, part // step, add_up, 0, unroll=True)


def first_kernel(count, nvec, slots, late, zs, swaps, where_at, rows, *refs):
    refs = list(refs)

    def take(n):
        head = refs[:n]
        del refs[:n]
        return head

    early = slots - len(late)
    walks = take(3)
    smalls = take(slots)
    mine = take(2 * early)
    other, joined = take(2)
    acc, diags, source, marks, late_coeff = refs
    me, core = where_at[0], where_at[1]
    per = 2 * count * nvec
    base = per * slots
    width = walks[0].shape[1]
    nelec = width // 2
    norb = walks[0].shape[2]
    half = norb // 2
    part = half // 2
    pad = source.shape[1] // 2

    def row_of(group):
        return group ^ me if swaps else group

    total = jnp.float32(0.0)
    before = jnp.float32(0.0)
    base_count = jnp.float32(0.0)
    for group in range(CORES * zs):
        at = row_of(jnp.int32(group))
        earlier = (group < me).astype(f32)
        for w in range(count):
            weight = rows[at, base + w]
            total += weight
            before += earlier * weight
            base_count += earlier * rows[at, base + count + w]
    for w in range(count):
        before += rows[row_of(me), base + w]
        marks[w] = (CORES * zs * count) * before / total

    lines, held = [], []
    for q in range(3):
        group = me + (q - 1)
        exists = (group >= 0) & (group < CORES * zs)
        lines.append(row_of(jnp.where(exists, group, me)))
        held.append(
            [jnp.where(exists, rows[lines[q], base + count + w], 0.0) for w in range(count)]
        )
    begin = base_count
    for w in range(count):
        begin -= held[0][w]
    line = [jnp.int32(0)] * count
    which = [jnp.int32(0)] * count
    place = [jnp.int32(0)] * count
    for q in range(3):
        at = jnp.int32(0) if q == 1 else jnp.where(core == (1 if q == 0 else 0), 1, 2)
        for w in range(count):
            end = begin + held[q][w]
            for j in range(count):
                slot = (me * count + j).astype(f32)
                chosen = (begin <= slot) & (slot < end)
                line[j] = jnp.where(chosen, lines[q], line[j])
                which[j] = jnp.where(chosen, w, which[j])
                place[j] = jnp.where(chosen, at, place[j])
            begin = end
    coeff = []
    for j in range(count):
        for ri in range(2):
            coeff.append(
                [
                    [
                        rows[line[j], slot * per + which[j] * 2 * nvec + 2 * g + ri]
                        for g in range(nvec)
                    ]
                    for slot in range(slots)
                ]
            )
        for k in range(3):

            @pl.when(place[j] == k)
            def _():
                source[j, :nelec] = walks[k][which[j], :nelec]
                source[j, pad : pad + nelec] = walks[k][which[j], nelec:]

        for lo in (nelec, pad + nelec):
            source[j, lo : lo + pad - nelec] = jnp.zeros((pad - nelec, norb), f32)

    for n in range(2 * count):
        for k, slot in enumerate(late):
            for g in range(nvec):
                late_coeff[n, k * nvec + g] = coeff[n][slot][g]
        diag = jnp.zeros((1, half), f32)
        for k in range(slots):
            for g in range(nvec):
                diag += coeff[n][k][g] * smalls[k][g + 1 : g + 2, :]
        diags[n : n + 1] = diag
    now = [[c[k] for k in range(slots) if k not in late] for c in coeff]
    size = nvec * part
    theirs = [other.at[0], other.at[1]]
    theirs += [joined.at[pl.ds(n * size, size)] for n in range(2 * early - 2)]
    for side, pieces in enumerate((mine, theirs)):
        at_half = core if side == 0 else CORES - 1 - core
        for p in range(2):
            add_pieces(acc, None, at_half, p, pieces[p::2], now, part, 32)


def last_kernel(count, nvec, late, where_at, late_coeff, early, diags, source, *refs):
    pieces, (out, acc, a_hi, a_lo) = list(refs[:-4]), refs[-4:]
    if late:
        joined = pieces.pop()
        size = joined.shape[0] // (2 * late)
        pieces += [joined.at[pl.ds(n * size, size)] for n in range(2 * late)]
    core = where_at[1]
    half = early.shape[2]
    part = half // 2
    pad = source.shape[1] // 2
    nelec = out.shape[1] // 2
    coeff = [
        [[late_coeff[n, k * nvec + g] for g in range(nvec)] for k in range(late)]
        for n in range(2 * count)
    ]
    for side in range(2):
        at_half = core if side == 0 else CORES - 1 - core
        for p in range(2):
            at = 2 * late * side + p
            add_pieces(acc, early, at_half, p, pieces[at : at + 2 * late : 2], coeff, part, 32)

    i, j_ = ids(half, half)

    def unpack(j):
        blocks = []
        for ri in range(2):
            diag = diags[2 * j + ri : 2 * j + ri + 1]
            square = acc[2 * j + ri, 0]
            turned = square.T
            corner = acc[2 * j + ri, 1]
            blocks.append(
                (
                    jnp.where(i <= j_, square, turned),
                    corner,
                    corner.T,
                    jnp.where(i > j_, square, jnp.where(i < j_, turned, diag)),
                )
            )
        for n in range(4):
            re, im = blocks[0][n], blocks[1][n]
            r, c = half * (n // 2), half * (n % 2)
            for k, value in enumerate((re, im - re, im + re)):
                hi = value.astype(jnp.bfloat16)
                a_hi[j, k, r : r + half, c : c + half] = hi
                a_lo[j, k, r : r + half, c : c + half] = (value - hi.astype(f32)).astype(jnp.bfloat16)

    terms = [source[j] for j in range(count)]
    series = list(terms)

    def advance(j, degree):
        term = terms[j]
        prods = []
        for n, left in enumerate((term[:pad] + term[pad:], term[:pad], term[pad:])):
            hi = left.astype(jnp.bfloat16)
            lo = (left - hi.astype(f32)).astype(jnp.bfloat16)
            wide = dot(jnp.concatenate([hi, lo], axis=0), a_hi[j, n])
            prods.append(wide[:pad] + wide[pad:] + dot(hi, a_lo[j, n]))
        terms[j] = jnp.concatenate([prods[0] - prods[2], prods[0] + prods[1]], axis=0) / degree
        series[j] = series[j] + terms[j]

    for j in range(count):
        unpack(j)
    for degree in range(1, TAYLOR + 1):
        for j in range(count):
            advance(j, degree)
    for j in range(count):
        out[j, :nelec] = series[j][:nelec]
        out[j, nelec:] = series[j][pad : pad + nelec]


def join_kernel(*refs):
    size = refs[0].shape[0]
    for n, ref in enumerate(refs[:-1]):
        refs[-1][n * size : (n + 1) * size] = ref[...]


def join(pieces, cost):
    rows, columns = pieces[0].shape
    return pl.pallas_call(
        join_kernel,
        out_shape=jax.ShapeDtypeStruct((len(pieces) * rows, columns), f32),
        in_specs=[VMEM] * len(pieces),
        out_specs=VMEM,
        compiler_params=PARAMS,
        cost_estimate=pl.CostEstimate(flops=cost, bytes_accessed=10, transcendentals=0),
    )(*pieces)


def after(value, *others):
    return lax.optimization_barrier((value, *others))[0]


def on_device(walkers, cholesky, fields, weights, counts):
    count, norb, width = walkers.shape
    nvec = cholesky.shape[0]
    half = norb // 2
    part = half // 2
    groups, shards = lax.axis_size("walk"), lax.axis_size("chol")
    zs = groups // CORES
    across = max(d for d in range(1, shards + 1) if shards % d == 0 and d * d <= shards)
    down = shards // across
    me = lax.axis_index("walk").astype(jnp.int32)
    core = me % CORES
    where_at = jnp.stack([me, core])

    def move(block, dy, dx):
        route = []
        for s in range(shards):
            y, x = divmod(s, across)
            route.append((s, (y + dy) % down * across + (x + dx) % across))
        return lax.ppermute(block, "chol", route)

    def to_core(block):
        return lax.ppermute(block, "walk", [(g, g ^ 1) for g in range(groups)])

    def over_edge(block):
        route = [(g, g + 1) for g in range(1, groups - 1, CORES)]
        ends = [(g, g) for g in (0, groups - 1)]
        return lax.ppermute(block, "walk", route + [(b, a) for a, b in route] + ends)

    order = [(dy, dx) for dy in range(down) for dx in range(across)]
    late = [k for k, (dy, dx) in enumerate(order) if dy and dx]
    walk_t = jnp.swapaxes(walkers, 1, 2)

    first, second, other, top, diags = pack(where_at, cholesky, up_to(width // 2, 8))
    got1, got2 = {(0, 0): first}, {(0, 0): second}
    for dx in range(1, across):
        got1[0, dx] = move(first, 0, dx)
    for dy in range(1, down):
        got2[dy, 0] = move(second, dy, 0)

    edge_walk = over_edge(after(walk_t, first))

    pad = up_to(width // 2, 128)
    small = pl.pallas_call(
        prep_kernel,
        out_shape=jax.ShapeDtypeStruct((SMALL, half), f32),
        in_specs=[SMEM] + [VMEM] * 3,
        out_specs=VMEM,
        scratch_shapes=[pltpu.VMEM((count, 2 * pad, norb), f32)],
        compiler_params=PARAMS,
        cost_estimate=pl.CostEstimate(flops=10**10, bytes_accessed=3 * 10**6, transcendentals=0),
    )(fields, walk_t, top, diags)
    smalls = [small if d == (0, 0) else move(small, *d) for d in order]
    for dx in range(1, across):
        got2[0, dx] = move(after(second, small, got1[0, dx]), 0, dx)
    for dy in range(1, down):
        got1[dy, 0] = move(after(first, small, got2[dy, 0]), dy, 0)
    for dy in range(1, down):
        for dx in range(1, across):
            got1[dy, dx] = move(got1[0, dx], dy, 0)
            got2[dy, dx] = move(got2[dy, 0], 0, dx)

    mine = [(got1[d], got2[d]) for d in order]
    joint = [p for k, two in enumerate(mine) for p in two if k and k not in late]
    core_walk = to_core(after(walk_t, small))
    row = pl.pallas_call(
        functools.partial(group_kernel, count, nvec),
        out_shape=jax.ShapeDtypeStruct((1, half), f32),
        in_specs=[SMEM, SMEM] + [VMEM] * shards,
        out_specs=VMEM,
        compiler_params=PARAMS,
        cost_estimate=pl.CostEstimate(flops=K2_COST, bytes_accessed=10, transcendentals=0),
    )(weights, counts, *smalls)
    swaps = groups & (groups - 1) == 0
    if swaps:
        rows = row
        for k in range(groups.bit_length() - 1):
            route = [(g, g ^ 2**k) for g in range(groups)]
            if k == EDGE_STEP:
                rows = after(rows, edge_walk)
            rows = jnp.concatenate([rows, lax.ppermute(rows, "walk", route)], axis=0)
            pair = rows if k < 2 else pair
    else:
        rows = pair = lax.all_gather(row, "walk", axis=0, tiled=True)
    joined = to_core(join([after(p, pair) for p in joint], EARLY_COST))
    my_late = [p for k in late for p in mine[k]]
    their_late = to_core(join([after(p, rows) for p in my_late], LATE_COST)) if late else None
    soon = [p for k, two in enumerate(mine) for p in two if k not in late] + [other, joined]
    epad = up_to(width // 2, 16)
    acc, diags, source, marks, late_coeff = pl.pallas_call(
        functools.partial(first_kernel, count, nvec, shards, late, zs, swaps),
        out_shape=(
            jax.ShapeDtypeStruct((2 * count, 2, half, half), f32),
            jax.ShapeDtypeStruct((up_to(2 * count, 8), half), f32),
            jax.ShapeDtypeStruct((count, 2 * epad, norb), f32),
            jax.ShapeDtypeStruct((count,), f32),
            jax.ShapeDtypeStruct((2 * count, max(1, len(late)) * nvec), f32),
        ),
        in_specs=[SMEM] * 2 + [VMEM] * (3 + shards + len(soon)),
        out_specs=(VMEM, VMEM, VMEM, SMEM, SMEM),
        compiler_params=PARAMS,
        cost_estimate=pl.CostEstimate(flops=K_COST, bytes_accessed=10, transcendentals=0),
    )(where_at, rows, walk_t, core_walk, edge_walk, *smalls, *soon)

    rest = my_late + ([their_late] if late else [])
    out = pl.pallas_call(
        functools.partial(last_kernel, count, nvec, len(late)),
        out_shape=jax.ShapeDtypeStruct((count, width, norb), f32),
        in_specs=[SMEM, SMEM] + [VMEM] * (3 + len(rest)),
        out_specs=VMEM,
        scratch_shapes=[
            pltpu.VMEM((2 * count, 2, half, half), f32),
            pltpu.VMEM((count, 3, norb, norb), jnp.bfloat16),
            pltpu.VMEM((count, 3, norb, norb), jnp.bfloat16),
        ],
        compiler_params=PARAMS,
        cost_estimate=pl.CostEstimate(flops=10**10, bytes_accessed=10**7, transcendentals=0),
    )(where_at, late_coeff, acc, diags, source, *rest)
    return jnp.swapaxes(out, 1, 2), marks


def solution(mesh):
    in_specs = (
        P("walk", None, None),
        P("chol", None, None),
        P("walk", "chol"),
        P("walk"),
        P("walk"),
    )
    out_specs = (P("walk", None, None), P("walk"))
    return jax.shard_map(
        on_device, mesh=mesh, in_specs=in_specs, out_specs=out_specs, check_vma=False
    )
```
